256 devices in a mesh: expert: 16 (over z_lo, x), dp: 16 (over y, z_hi, core).
Axes of the slice: x: 4, y: 4, z: 8 (z_hi: 2, z_lo: 4; z = z_hi * 4 + z_lo), core: 2. Of those that a mesh axis runs over, the one named last changes fastest.
Arguments:
- queries: bfloat16 [32768, 18432], P(('expert', 'dp')), may hold values from -32 to 32
- new_latent: bfloat16 [32768, 576], P(('expert', 'dp')), may hold values from -4 to 4
- held_pages: bfloat16 [16, 128, 36864], P('expert', 'dp'), may hold values from -4 to 4
- page_list: int32 [256, 16], P(('expert', 'dp')), may hold values from 0 to 127, as said below
- token_expert: int32 [32768, 1], P(('expert', 'dp')), may hold values from 0 to 383, as said below
- gate: float32 [32768, 1], P(('expert', 'dp')), may hold values from 0.3 to 3
- expert_rows: bfloat16 [16, 16, 16, 9, 7168], P('expert', 'dp'), may hold values from -6 to 6
- page_table: int32 [16, 32], P('expert', 'dp'), may hold values from 0 to 31, each once within a row
Outputs:
- context: bfloat16 [32768, 16384], P(('expert', 'dp'))
- moe_out: bfloat16 [32768, 7168], P(('expert', 'dp'))
- decode_pool: bfloat16 [16, 32, 36864], P('expert', 'dp')
The draws below stay inside these ranges and needn't reach their ends.
Inputs may be any that keep to these rules, and one draw needn't show every extreme that they name: `page_list`: each span lists 16 distinct pages of its pool, at most 2 from the 8 pages of one holder (holder = page // 8), and exactly 2 from at least one holder. `token_expert`: for every span, at most 9 of its (token, slot) pairs name experts of one expert index (expert // 24), and exactly 9 for some index. `page_table`: each row is a permutation.
All inputs are finite; a program needn't handle non-finite values.
Results may differ from the reference program's by a relative error of at most 0.012.
Values may be sent and summed in bfloat16 or wider, within the bound.
No kernel may reach another device: no remote copies, remote signals or barrier semaphores. Data moves between devices by JAX's collectives and lax.ppermute only.
A program may use at most 128 MiB of HBM per device.

```python
import math
import jax
import jax.numpy as jnp
from jax import lax

D = 7168
EXP_GROUP = 24
H = 32
LAT = 512
ROPE = 64
PAGE = 64
TOK = 128
SLOTS = 1
HELD = 8
LIST = 16
CAP = 9
NEWP = 2
TOKENS = 32768
N_EXPERT = 16
N_DP = 16


def shared_latent(key):
    return jnp.clip(jax.random.normal(key, (TOKENS, LAT + ROPE), jnp.float32), -4.0, 4.0)


def draw_new_latent(key, part):
    shared = shared_latent(key)
    return shared.astype(jnp.bfloat16)


def draw_queries(key, part):
    key = jax.random.fold_in(key, 2)
    values = jnp.clip(jax.random.normal(key, (TOKENS, H, LAT + ROPE), jnp.float32), -4.0, 4.0)
    return values.reshape(TOKENS, H * (LAT + ROPE)).astype(jnp.bfloat16)


def draw_page_list(key, part):
    key = jax.random.fold_in(key, 3)
    doubled = max(1, LIST - N_DP)
    single = LIST - 2 * doubled
    distinct = doubled + single

    def held_order(subkey):
        return jax.random.permutation(subkey, HELD)

    def one_span(subkey):
        key_holders, key_pages, key_order = jax.random.split(subkey, 3)
        holders = jax.random.permutation(key_holders, N_DP)
        orders = jax.vmap(held_order)(jax.random.split(key_pages, N_DP))
        entries = jnp.concatenate([holders[:distinct], holders[:doubled]])
        repeat_flag = jnp.concatenate([jnp.zeros((distinct,), jnp.int32), jnp.ones((doubled,), jnp.int32)])
        within = orders[entries, repeat_flag]
        listed = entries * HELD + within
        return listed[jax.random.permutation(key_order, LIST)]
    return jax.vmap(one_span)(jax.random.split(key, N_EXPERT * N_DP)).astype(jnp.int32)


def draw_token_expert(key, part):
    key = jax.random.fold_in(key, 4)
    slot_count = TOK * SLOTS

    def one_span(subkey):
        key_target, key_giving, key_order, key_member = jax.random.split(subkey, 4)
        groups = jnp.arange(slot_count, dtype=jnp.int32) % N_EXPERT
        target = jax.random.randint(key_target, (), 0, N_EXPERT)
        giving = (target + jax.random.randint(key_giving, (), 1, N_EXPERT)) % N_EXPERT
        groups = jnp.where(jnp.arange(slot_count, dtype=jnp.int32) == giving, target, groups)
        groups = groups[jax.random.permutation(key_order, slot_count)]
        return groups * EXP_GROUP + jax.random.randint(key_member, (slot_count,), 0, EXP_GROUP)
    chosen = jax.vmap(one_span)(jax.random.split(key, N_EXPERT * N_DP))
    return chosen.reshape(TOKENS, SLOTS).astype(jnp.int32)


def levels(rng, shape, cuts, smallest, high):
    loudness = 1.0
    for position, parts in cuts:
        heights = jax.random.uniform(jax.random.fold_in(jax.random.fold_in(rng, 6), position), (parts,), jnp.float32, smallest / len(cuts), high / len(cuts))
        loudness = loudness * jnp.repeat(jnp.exp(heights), shape[position] // parts).reshape((-1,) + (1,) * (len(shape) - 1 - position))
    return loudness


def noise(key, dims, width, bound, shards=(), held_as=jnp.bfloat16):
    values = width * jax.random.normal(key, dims, jnp.float32)
    if shards:
        values = values * levels(key, dims, shards, -0.22, 0.18)
    return jnp.clip(values, -bound, bound).astype(held_as)


def setup_inputs(seed: int = 0) -> dict:
    splits = jax.random.split(jax.random.key(seed), 9)
    return {
        "queries": draw_queries(jax.random.fold_in(splits[8], 71), 0),
        "new_latent": draw_new_latent(jax.random.fold_in(splits[8], 71), 0),
        "held_pages": noise(splits[2], (N_EXPERT, N_DP * HELD, PAGE * (LAT + ROPE)), 1.0, 4.0, ((0, 16), (1, 16))),
        "page_list": draw_page_list(jax.random.fold_in(splits[8], 71), 0),
        "token_expert": draw_token_expert(jax.random.fold_in(splits[8], 71), 0),
        "gate": jnp.clip(jnp.exp(math.log(3.0) - 2.3025851 * jax.random.uniform(splits[5], (TOKENS, SLOTS), jnp.float32) ** levels(splits[5], (TOKENS, SLOTS), ((0, 256),), -0.2, 0.2)), 0.3, 3.0),
        "expert_rows": noise(splits[6], (N_EXPERT, N_DP, N_EXPERT, CAP, D), 1.0, 6.0, ((0, 16), (1, 16))),
        "page_table": jax.vmap(lambda own: jax.random.permutation(own, N_DP * NEWP))(jax.random.split(splits[7], N_EXPERT)).reshape((N_EXPERT, N_DP * NEWP)).astype(jnp.int32),
    }


score_scale = 0.07216878364870322


def attend(queries, key_rows):
    tokens_here = queries.shape[0]
    key_width = key_rows.shape[1]
    head_count = queries.shape[1] // key_width
    query_heads = queries.reshape(tokens_here, head_count, key_width).astype(jnp.float32)
    scores = jnp.einsum("thc,kc->htk", query_heads, key_rows.astype(jnp.float32)) * score_scale
    prefix = key_rows.shape[0] - tokens_here
    allowed = (jnp.arange(key_rows.shape[0])[None, :] - prefix) <= jnp.arange(tokens_here)[:, None]
    scores = jnp.where(allowed[None], scores, -jnp.inf)
    largest = jnp.max(scores, axis=2, keepdims=True)
    weights = jnp.exp(scores - largest)
    probabilities = (weights / jnp.sum(weights, axis=2, keepdims=True)).astype(jnp.bfloat16)
    context = jnp.einsum("htk,kc->thc", probabilities.astype(jnp.float32), key_rows[:, :LAT].astype(jnp.float32))
    return context.astype(jnp.bfloat16).reshape(tokens_here, head_count * LAT)


def reference(queries, new_latent, held_pages, page_list, token_expert, gate, expert_rows, page_table):
    spans = N_EXPERT * N_DP
    query_spans = queries.reshape(spans, TOK, -1)
    latent_spans = new_latent.reshape(spans, TOK, -1)

    def one_span(span_index):
        column = span_index // N_DP
        listed = page_list[span_index]
        page_rows = jnp.take(held_pages[column], listed, axis=0)
        key_rows = jnp.concatenate([page_rows.reshape(LIST * PAGE, LAT + ROPE), latent_spans[span_index]], axis=0)
        return attend(query_spans[span_index], key_rows)

    context = lax.map(one_span, jnp.arange(spans, dtype=jnp.int32)).reshape(TOKENS, H * LAT)

    groups = (token_expert // EXP_GROUP).reshape(spans, TOK * SLOTS)
    onehot = (groups[:, :, None] == jnp.arange(N_EXPERT, dtype=jnp.int32)[None, None, :]).astype(jnp.int32)
    ranking = jnp.sum((jnp.cumsum(onehot, axis=1) - onehot) * onehot, axis=2)
    owners = (jnp.arange(spans, dtype=jnp.int32) // N_DP)[:, None]
    dp_index = (jnp.arange(spans, dtype=jnp.int32) % N_DP)[:, None]
    picked = expert_rows[groups, dp_index, owners, ranking].astype(jnp.float32)
    weighted = picked.reshape(spans, TOK, SLOTS, D) * gate.reshape(spans, TOK, SLOTS, 1)
    moe_out = jnp.sum(weighted, axis=2).reshape(TOKENS, D).astype(jnp.bfloat16)

    pages_all = new_latent.reshape(N_EXPERT, N_DP * NEWP, PAGE * (LAT + ROPE))
    inverse = jnp.argsort(page_table, axis=1).astype(jnp.int32)
    decode_pool = jnp.take_along_axis(pages_all, inverse[:, :, None], axis=1)
    return context, moe_out, decode_pool
```

```python
import functools

import jax
import jax.numpy as jnp
from jax import lax
from jax.experimental import pallas as pl
from jax.experimental.pallas import tpu as pltpu
from jax.sharding import PartitionSpec as P

EXP_GROUP = 24
LAT = 512
PAIR = 2
LANES = 128

exp2_scale = 0.07216878364870322 * 1.4426950408889634


def pick_pages(pages, index):
    count = index.shape[0]

    def kernel(index_ref, pages_ref, out_ref, sems):
        def move(i):
            return pltpu.make_async_copy(pages_ref.at[index_ref[i]], out_ref.at[i], sems.at[i])

        for i in range(count):
            move(i).start()
        for i in range(count):
            move(i).wait()

    return pl.pallas_call(
        kernel,
        out_shape=jax.ShapeDtypeStruct((count,) + pages.shape[1:], pages.dtype),
        in_specs=[pl.BlockSpec(memory_space=pltpu.SMEM), pl.BlockSpec(memory_space=pl.ANY)],
        out_specs=pl.BlockSpec(memory_space=pl.ANY),
        scratch_shapes=[pltpu.SemaphoreType.DMA((count,))],
        name="pick_pages",
    )(index, pages)


def attend_kernel(step_pairs, width, place_ref, q_ref, own_ref, near_ref, far_ref, out_ref, held, low, high, sems):
    count, page_rows, pair_width = held.shape
    span = low.shape[1]
    shift = span - width
    tokens = own_ref.shape[0]
    half = count * page_rows
    prefix = 2 * half

    @pl.when(pl.program_id(0) == 0)
    def _():
        def start(i, source):
            place = place_ref[1, i]
            pltpu.make_async_copy(source.at[place], held.at[i], sems.at[i]).start()

        for i in range(count):

            @pl.when(place_ref[0, i] == 0)
            def _():
                start(i, near_ref)

            @pl.when(place_ref[0, i] != 0)
            def _():
                start(i, far_ref)

        own = own_ref[...]
        empty = jnp.zeros((tokens, shift), own.dtype)
        low[prefix:, :] = jnp.concatenate([own, empty], axis=1)
        high[prefix:, :] = jnp.concatenate([empty, own], axis=1)
        lane = lax.broadcasted_iota(jnp.int32, (page_rows, span), 1)
        for i in range(count):
            pltpu.make_async_copy(near_ref.at[0], held.at[i], sems.at[i]).wait()
            first = jnp.where(lane < width, held[i, :, :span].astype(jnp.float32), 0.0)
            second = jnp.where(lane >= shift, held[i, :, pair_width - span :].astype(jnp.float32), 0.0)
            evens = pl.ds(i * page_rows, page_rows)
            odds = pl.ds(half + i * page_rows, page_rows)
            low[evens, :] = first.astype(low.dtype)
            high[evens, :] = pltpu.roll(first, shift, 1).astype(low.dtype)
            low[odds, :] = pltpu.roll(second, width, 1).astype(low.dtype)
            high[odds, :] = second.astype(low.dtype)

    contract = (((1,), (1,)), ((), ()))
    rows = step_pairs * tokens
    token = lax.broadcasted_iota(jnp.int32, (rows, tokens), 0) % tokens
    visible = lax.broadcasted_iota(jnp.int32, (rows, tokens), 1) <= token
    for parity, keys in ((0, low), (1, high)):
        offset = parity * (pair_width - span)
        q = jnp.concatenate(
            [q_ref[:, p * pair_width + offset : p * pair_width + offset + span] for p in range(step_pairs)], axis=0
        )
        before = lax.dot_general(q, keys[:prefix, :], contract, preferred_element_type=jnp.float32)
        own = lax.dot_general(q, keys[prefix:, :], contract, preferred_element_type=jnp.float32)
        own = jnp.where(visible, own, -jnp.inf)
        largest = jnp.maximum(jnp.max(before, axis=1, keepdims=True), jnp.max(own, axis=1, keepdims=True))
        before = jnp.exp2((before - largest) * exp2_scale)
        own = jnp.exp2((own - largest) * exp2_scale)
        total = jnp.sum(before, axis=1, keepdims=True) + jnp.sum(own, axis=1, keepdims=True)
        mixed = jnp.dot(before.astype(low.dtype), low[:prefix, :LAT], preferred_element_type=jnp.float32)
        mixed += jnp.dot(own.astype(low.dtype), low[prefix:, :LAT], preferred_element_type=jnp.float32)
        mixed = (mixed / total).astype(out_ref.dtype)
        for p in range(step_pairs):
            head = 2 * p + parity
            out_ref[:, head * LAT : (head + 1) * LAT] = mixed[p * tokens : (p + 1) * tokens]


def attend(queries, own, near, far, place):
    tokens, width = own.shape
    _, page_rows, pair_width = near.shape
    count = place.shape[1]
    span = -(-width // LANES) * LANES
    pairs = queries.shape[1] // pair_width
    step_pairs = 2
    keys = count * page_rows * 2 + tokens
    heads = 2 * pairs
    return pl.pallas_call(
        functools.partial(attend_kernel, step_pairs, width),
        out_shape=jax.ShapeDtypeStruct((tokens, heads * LAT), queries.dtype),
        grid=(pairs // step_pairs,),
        in_specs=[
            pl.BlockSpec(memory_space=pltpu.SMEM),
            pl.BlockSpec((tokens, step_pairs * pair_width), lambda i: (0, i)),
            pl.BlockSpec((tokens, width), lambda i: (0, 0)),
            pl.BlockSpec(memory_space=pl.ANY),
            pl.BlockSpec(memory_space=pl.ANY),
        ],
        out_specs=pl.BlockSpec((tokens, 2 * step_pairs * LAT), lambda i: (0, i)),
        scratch_shapes=[
            pltpu.VMEM((count, page_rows, pair_width), queries.dtype),
            pltpu.VMEM((keys, span), queries.dtype),
            pltpu.VMEM((keys, span), queries.dtype),
            pltpu.SemaphoreType.DMA((count,)),
        ],
        compiler_params=pltpu.CompilerParams(vmem_limit_bytes=40 * 2**20),
        cost_estimate=pl.CostEstimate(
            flops=2 * tokens * heads * keys * (width + LAT),
            bytes_accessed=2 * tokens * heads * (width + LAT),
            transcendentals=tokens * heads * keys,
        ),
        name="attend",
    )(place, queries, own, near, far)


def combine_kernel(parts, slot_ref, gate_ref, rows_ref, out_ref):
    tokens = slot_ref.shape[0]
    depth, part_width = rows_ref.shape
    column = lax.broadcasted_iota(jnp.int32, (tokens, depth), 1)
    first = slot_ref[...] * parts
    picker = jnp.concatenate(
        [(column == first + part).astype(rows_ref.dtype) for part in range(parts)], axis=0
    )
    picked = jnp.dot(picker, rows_ref[...], preferred_element_type=jnp.float32)
    gate = gate_ref[...]
    for part in range(parts):
        out_ref[:, part * part_width : (part + 1) * part_width] = (
            picked[part * tokens : (part + 1) * tokens] * gate
        ).astype(out_ref.dtype)


def combine(slot, gate, arrived, parts):
    tokens = slot.shape[0]
    depth, part_width = arrived.shape
    return pl.pallas_call(
        functools.partial(combine_kernel, parts),
        out_shape=jax.ShapeDtypeStruct((tokens, parts * part_width), arrived.dtype),
        in_specs=[pl.BlockSpec(memory_space=pltpu.VMEM)] * 3,
        out_specs=pl.BlockSpec(memory_space=pltpu.VMEM),
        compiler_params=pltpu.CompilerParams(vmem_limit_bytes=40 * 2**20),
        cost_estimate=pl.CostEstimate(
            flops=2 * parts * tokens * depth * part_width,
            bytes_accessed=2 * (depth + tokens * parts) * part_width,
            transcendentals=0,
        ),
        name="combine",
    )(slot, gate, arrived)


def earlier_same(groups):
    count = groups.shape[0]
    order = jnp.arange(count, dtype=jnp.int32)
    same = (groups[None, :] == groups[:, None]) & (order[None, :] < order[:, None])
    return jnp.sum(same.astype(jnp.int32), axis=1)


def shards(queries, new_latent, held_pages, page_list, token_expert, gate, expert_rows, page_table):
    groups_here = lax.axis_size("expert")
    dp_size = lax.axis_size("dp")
    me = lax.axis_index("dp")
    held_count, page_width = held_pages.shape[1:]
    entry_width = new_latent.shape[1]
    pair_width = 2 * entry_width
    page_rows = page_width // pair_width
    half_of = lambda i: (i // 2) % 2
    seat_of = lambda i: (i // 4) * 2 + i % 2
    halves = [[i for i in range(dp_size) if half_of(i) == z] for z in range(2)]
    across = [(i, i ^ 2) for i in range(dp_size)]
    seats = dp_size // 2

    raw = held_pages[0]
    raw_far = lax.ppermute(raw, "dp", across)

    listed = page_list.reshape(-1)
    count = listed.shape[0]
    lists = lax.all_to_all(
        jnp.broadcast_to(listed[None], (seats, count)), "dp", 0, 0, axis_index_groups=halves, tiled=True
    )

    order = jnp.arange(count, dtype=jnp.int32)

    def chosen(holder):
        mine = (lists // held_count) == holder
        rank = jnp.sum((mine[:, None, :] & (order[None, None, :] < order[None, :, None])).astype(jnp.int32), axis=2)
        slots = jnp.arange(PAIR, dtype=jnp.int32)
        hit = mine[:, None, :] & (rank[:, None, :] == slots[None, :, None])
        return jnp.sum(jnp.where(hit, (lists % held_count)[:, None, :], 0), axis=2).reshape(-1)

    def deliver(pages, holder):
        picked = pick_pages(pages.reshape(held_count, page_rows, pair_width), chosen(holder))
        blocks = picked.reshape(seats, PAIR * page_rows, pair_width)
        arrived = lax.all_to_all(blocks, "dp", 0, 0, axis_index_groups=halves, tiled=True)
        return arrived.reshape(seats * PAIR, page_rows, pair_width)

    near = deliver(raw, me)

    capacity, width = expert_rows.shape[3:]
    parts = 8
    blocks = expert_rows.reshape(groups_here, capacity * parts, width // parts)
    blocks, lists = lax.optimization_barrier((blocks, lists))
    arrived = lax.all_to_all(blocks, "expert", 0, 0, tiled=True)

    far = deliver(raw_far, me ^ 2)

    holders = listed // held_count
    rank = jnp.minimum(earlier_same(holders), PAIR - 1)
    place = jnp.stack([(half_of(holders) != half_of(me)).astype(jnp.int32), seat_of(holders) * PAIR + rank])
    context = attend(queries, new_latent, near, far, place)

    groups = (token_expert // EXP_GROUP).reshape(-1)
    slot = groups * capacity + earlier_same(groups)
    moe_out = combine(
        slot[:, None], gate, arrived.reshape(groups_here * capacity * parts, width // parts), parts
    )

    new_count = page_table.shape[1]
    tags = jnp.broadcast_to(page_table.reshape(new_count, 1).astype(new_latent.dtype), (new_count, LANES))
    tagged = jnp.concatenate([new_latent.reshape(new_count, page_width), tags], axis=1)
    pages = lax.all_gather(tagged, "dp", axis=0, tiled=True)
    targets = pages[:, page_width].astype(jnp.int32)
    wanted = me * new_count + jnp.arange(new_count, dtype=jnp.int32)
    picker = (wanted[:, None] == targets[None, :]).astype(pages.dtype)
    slots = jnp.dot(picker, pages[:, :page_width], preferred_element_type=jnp.float32)
    decode_pool = slots.astype(pages.dtype).reshape(1, new_count, page_width)
    return (context, moe_out, decode_pool)


def solution(mesh):
    return jax.shard_map(
        shards,
        mesh=mesh,
        in_specs=(
            P(("expert", "dp"), None),
            P(("expert", "dp"), None),
            P("expert", "dp", None),
            P(("expert", "dp"), None),
            P(("expert", "dp"), None),
            P(("expert", "dp"), None),
            P("expert", "dp", None, None, None),
            P("expert", "dp"),
        ),
        out_specs=(P(("expert", "dp"), None), P(("expert", "dp"), None), P("expert", "dp", None)),
        check_vma=False,
    )
```

```python
import functools

import jax
import jax.numpy as jnp
from jax import lax
from jax.experimental import pallas as pl
from jax.experimental.pallas import tpu as pltpu
from jax.sharding import PartitionSpec as P

EXP_GROUP = 24
LAT = 512
PAIR = 2
LANES = 128

exp2_scale = 0.07216878364870322 * 1.4426950408889634


def pick_kernel(index_ref, *refs):
    page_refs, out_ref = refs[:-1], refs[-1]
    each, count = len(page_refs), index_ref.shape[0]
    for i in range(count):
        out_ref[i] = page_refs[i // PAIR % each][index_ref[i], : out_ref.shape[1]]


def pick_pages(sources, index, rows=None):
    width = sources[0].shape[2]
    rows = rows or sources[0].shape[1]
    return pl.pallas_call(
        pick_kernel,
        out_shape=jax.ShapeDtypeStruct((index.shape[0], rows, width), sources[0].dtype),
        in_specs=[pl.BlockSpec(memory_space=pltpu.SMEM)] + [pl.BlockSpec(memory_space=pltpu.VMEM)] * len(sources),
        out_specs=pl.BlockSpec(memory_space=pltpu.VMEM),
        compiler_params=pltpu.CompilerParams(vmem_limit_bytes=16 * 2**20),
        name="pick_pages",
    )(index, *sources)


def attend_kernel(step_pairs, width, blocks, place_ref, q_ref, own_ref, *refs):
    block_refs, (out_ref, held, low, high, sems) = refs[:blocks], refs[blocks:]
    count = place_ref.shape[0]
    each, page_rows, pair_width = block_refs[0].shape
    span = low.shape[1]
    shift = span - width
    tokens = own_ref.shape[0]
    half = count * page_rows
    prefix = 2 * half

    @pl.when(pl.program_id(0) == 0)
    def _():
        def move(i):
            return pltpu.make_async_copy(block_refs[i], held.at[pl.ds(each * i, each)], sems.at[i])

        for i in range(blocks):
            move(i).start()

        own = own_ref[...]
        empty = jnp.zeros((tokens, shift), own.dtype)
        low[prefix:, :] = jnp.concatenate([own, empty], axis=1)
        high[prefix:, :] = jnp.concatenate([empty, own], axis=1)
        lane = lax.broadcasted_iota(jnp.int32, (page_rows, span), 1)
        for i in range(blocks):
            move(i).wait()
        for i in range(count):
            place = place_ref[i]
            first = jnp.where(lane < width, held[place, :, :span].astype(jnp.float32), 0.0)
            second = jnp.where(lane >= shift, held[place, :, pair_width - span :].astype(jnp.float32), 0.0)
            evens = pl.ds(i * page_rows, page_rows)
            odds = pl.ds(half + i * page_rows, page_rows)
            low[evens, :] = first.astype(low.dtype)
            high[evens, :] = pltpu.roll(first, shift, 1).astype(low.dtype)
            low[odds, :] = pltpu.roll(second, width, 1).astype(low.dtype)
            high[odds, :] = second.astype(low.dtype)

    contract = (((1,), (1,)), ((), ()))
    rows = step_pairs * tokens
    token = lax.broadcasted_iota(jnp.int32, (rows, tokens), 0) % tokens
    visible = lax.broadcasted_iota(jnp.int32, (rows, tokens), 1) <= token
    for parity, keys in ((0, low), (1, high)):
        offset = parity * (pair_width - span)
        q = jnp.concatenate(
            [q_ref[:, p * pair_width + offset : p * pair_width + offset + span] for p in range(step_pairs)], axis=0
        )
        before = lax.dot_general(q, keys[:prefix, :], contract, preferred_element_type=jnp.float32)
        own = lax.dot_general(q, keys[prefix:, :], contract, preferred_element_type=jnp.float32)
        own = jnp.where(visible, own, -jnp.inf)
        largest = jnp.maximum(jnp.max(before, axis=1, keepdims=True), jnp.max(own, axis=1, keepdims=True))
        before = jnp.exp2((before - largest) * exp2_scale)
        own = jnp.exp2((own - largest) * exp2_scale)
        total = jnp.sum(before, axis=1, keepdims=True) + jnp.sum(own, axis=1, keepdims=True)
        mixed = jnp.dot(before.astype(low.dtype), low[:prefix, :LAT], preferred_element_type=jnp.float32)
        mixed += jnp.dot(own.astype(low.dtype), low[prefix:, :LAT], preferred_element_type=jnp.float32)
        mixed = (mixed / total).astype(out_ref.dtype)
        for p in range(step_pairs):
            head = 2 * p + parity
            out_ref[:, head * LAT : (head + 1) * LAT] = mixed[p * tokens : (p + 1) * tokens]


def attend(queries, own, blocks, place):
    tokens, width = own.shape
    _, page_rows, pair_width = blocks[0].shape
    count = place.shape[0]
    span = -(-width // LANES) * LANES
    pairs = queries.shape[1] // pair_width
    step_pairs = 4
    keys = count * page_rows * 2 + tokens
    heads = 2 * pairs
    return pl.pallas_call(
        functools.partial(attend_kernel, step_pairs, width, len(blocks)),
        out_shape=jax.ShapeDtypeStruct((tokens, heads * LAT), queries.dtype),
        grid=(pairs // step_pairs,),
        in_specs=[
            pl.BlockSpec(memory_space=pltpu.SMEM),
            pl.BlockSpec((tokens, step_pairs * pair_width), lambda i: (0, i)),
            pl.BlockSpec((tokens, width), lambda i: (0, 0)),
        ]
        + [pl.BlockSpec(memory_space=pl.ANY)] * len(blocks),
        out_specs=pl.BlockSpec((tokens, 2 * step_pairs * LAT), lambda i: (0, i)),
        scratch_shapes=[
            pltpu.VMEM((len(blocks) * blocks[0].shape[0], page_rows, pair_width), queries.dtype),
            pltpu.VMEM((keys, span), queries.dtype),
            pltpu.VMEM((keys, span), queries.dtype),
            pltpu.SemaphoreType.DMA((len(blocks),)),
        ],
        compiler_params=pltpu.CompilerParams(vmem_limit_bytes=56 * 2**20),
        cost_estimate=pl.CostEstimate(
            flops=2 * tokens * heads * keys * (width + LAT),
            bytes_accessed=2 * tokens * heads * (width + LAT),
            transcendentals=tokens * heads * keys,
        ),
        name="attend",
    )(place, queries, own, *blocks)


def pack_kernel(groups, parts, here_ref, rows_ref, *refs):
    out_refs, stack = refs[:-1], refs[-1]
    count, width = rows_ref.shape
    part_width = width // parts
    for part in range(parts):
        stack[pl.ds(part * count, count), :] = rows_ref[:, part * part_width : (part + 1) * part_width]
    side = len(out_refs)
    block = count // groups * parts
    depth = parts * count
    row = lax.broadcasted_iota(jnp.int32, (side * block, 1), 0)
    k = row // block
    slot = (row - k * block) // parts
    part = row % parts
    column = lax.broadcasted_iota(jnp.int32, (side * block, depth), 1)
    for far in range(side):
        group = (k * side + far) ^ here_ref[0]
        picker = (column == part * count + slot * groups + group).astype(stack.dtype)
        out_refs[far][...] = jnp.dot(picker, stack[...], preferred_element_type=jnp.float32).astype(stack.dtype)


def pack_rows(rows, here, groups, side, parts):
    count, width = rows.shape
    out = jax.ShapeDtypeStruct((count * parts // side, width // parts), rows.dtype)
    return pl.pallas_call(
        functools.partial(pack_kernel, groups, parts),
        out_shape=(out,) * side,
        in_specs=[pl.BlockSpec(memory_space=pltpu.SMEM), pl.BlockSpec(memory_space=pltpu.VMEM)],
        out_specs=(pl.BlockSpec(memory_space=pltpu.VMEM),) * side,
        scratch_shapes=[pltpu.VMEM((count * parts, width // parts), rows.dtype)],
        compiler_params=pltpu.CompilerParams(vmem_limit_bytes=32 * 2**20),
        cost_estimate=pl.CostEstimate(
            flops=2 * count * parts * count * width, bytes_accessed=4 * count * width, transcendentals=0
        ),
        name="pack_rows",
    )(here, rows)


def turn_kernel(*refs):
    side = len(refs) // 2
    share = refs[0].shape[0] // side
    for k in range(side):
        for far in range(side):
            refs[side + k][pl.ds(far * share, share), :] = refs[far][pl.ds(k * share, share), :]


def turn(blocks):
    side = len(blocks)
    return pl.pallas_call(
        turn_kernel,
        out_shape=(jax.ShapeDtypeStruct(blocks[0].shape, blocks[0].dtype),) * side,
        in_specs=[pl.BlockSpec(memory_space=pltpu.VMEM)] * side,
        out_specs=(pl.BlockSpec(memory_space=pltpu.VMEM),) * side,
        compiler_params=pltpu.CompilerParams(vmem_limit_bytes=16 * 2**20),
        name="turn",
    )(*blocks)


def combine_kernel(parts, slot_ref, gate_ref, *refs):
    row_refs, (out_ref, rows, sems) = refs[:-3], refs[-3:]
    tokens = slot_ref.shape[0]
    depth, part_width = rows.shape
    share = row_refs[0].shape[0]

    def move(i):
        return pltpu.make_async_copy(row_refs[i], rows.at[pl.ds(i * share, share)], sems.at[i])

    for i in range(len(row_refs)):
        move(i).start()
    column = lax.broadcasted_iota(jnp.int32, (tokens, depth), 1)
    first = slot_ref[...] * parts
    picker = jnp.concatenate([(column == first + part).astype(rows.dtype) for part in range(parts)], axis=0)
    gate = gate_ref[...]
    for i in range(len(row_refs)):
        move(i).wait()
    picked = jnp.dot(picker, rows[...], preferred_element_type=jnp.float32)
    for part in range(parts):
        out_ref[:, part * part_width : (part + 1) * part_width] = (
            picked[part * tokens : (part + 1) * tokens] * gate
        ).astype(out_ref.dtype)


def combine(slot, gate, arrived, parts):
    tokens = slot.shape[0]
    depth = sum(block.shape[0] for block in arrived)
    part_width = arrived[0].shape[1]
    return pl.pallas_call(
        functools.partial(combine_kernel, parts),
        out_shape=jax.ShapeDtypeStruct((tokens, parts * part_width), arrived[0].dtype),
        in_specs=[pl.BlockSpec(memory_space=pltpu.VMEM)] * 2 + [pl.BlockSpec(memory_space=pl.ANY)] * len(arrived),
        out_specs=pl.BlockSpec(memory_space=pltpu.VMEM),
        scratch_shapes=[
            pltpu.VMEM((depth, part_width), arrived[0].dtype),
            pltpu.SemaphoreType.DMA((len(arrived),)),
        ],
        compiler_params=pltpu.CompilerParams(vmem_limit_bytes=40 * 2**20),
        cost_estimate=pl.CostEstimate(
            flops=2 * parts * tokens * depth * part_width,
            bytes_accessed=2 * (depth + tokens * parts) * part_width,
            transcendentals=0,
        ),
        name="combine",
    )(slot, gate, *arrived)


def earlier_same(groups):
    count = groups.shape[0]
    order = jnp.arange(count, dtype=jnp.int32)
    same = (groups[None, :] == groups[:, None]) & (order[None, :] < order[:, None])
    return jnp.sum(same.astype(jnp.int32), axis=1)


def first_match(wanted, values):
    hit = wanted[:, None] == values[None, :]
    order = jnp.arange(values.shape[0], dtype=jnp.int32)
    first = jnp.min(jnp.where(hit, order[None, :], values.shape[0]), axis=1)
    return jnp.where(first < values.shape[0], first, 0)


def shards(queries, new_latent, held_pages, page_list, token_expert, gate, expert_rows, page_table):
    groups_here = lax.axis_size("expert")
    dp_size = lax.axis_size("dp")
    me = lax.axis_index("dp")
    held_count, page_width = held_pages.shape[1:]
    entry_width = new_latent.shape[1]
    pair_width = 2 * entry_width
    page_rows = page_width // pair_width
    half_of = lambda i: (i // 2) % 2
    seat_of = lambda i: (i // 4) * 2 + i % 2
    halves = [[i for i in range(dp_size) if half_of(i) == z] for z in range(2)]
    across = [(i, i ^ 2) for i in range(dp_size)]
    seats = dp_size // 2

    raw = held_pages[0]
    raw_far = lax.ppermute(raw, "dp", across)

    listed = page_list.reshape(-1)
    count = listed.shape[0]
    here = lax.axis_index("expert")
    capacity, width = expert_rows.shape[3:]
    parts = 8
    side = 4
    along = lambda k: [(i, i ^ k) for i in range(groups_here)]
    rows = jnp.transpose(expert_rows[0, 0], (1, 0, 2)).reshape(capacity * groups_here, width)
    packed = pack_rows(rows, here.reshape(1).astype(jnp.int32), groups_here, side, parts)
    packed, listed = lax.optimization_barrier((packed, listed))
    lists = lax.all_to_all(
        jnp.broadcast_to(listed[None], (seats, count)), "dp", 0, 0, axis_index_groups=halves, tiled=True
    )

    order = jnp.arange(count, dtype=jnp.int32)
    mine = (lists // held_count)[:, None, :] == jnp.stack([me, me ^ 2])[None, :, None]
    rank = jnp.sum((mine[:, :, None, :] & (order[None, :] < order[:, None])).astype(jnp.int32), axis=3)
    slots = jnp.arange(PAIR, dtype=jnp.int32)
    hit = mine[:, :, None, :] & (rank[:, :, None, :] == slots[:, None])
    chosen = jnp.sum(jnp.where(hit, (lists % held_count)[:, None, None, :], 0), axis=3).reshape(-1)

    def deliver(picked):
        blocks = picked.reshape(seats, -1, picked.shape[2])
        arrived = lax.all_to_all(blocks, "dp", 0, 0, axis_index_groups=halves, tiled=True)
        return arrived.reshape(picked.shape)

    met = [packed[0]] + [lax.ppermute(packed[far], "expert", along(far)) for far in range(1, side)]
    page_shape = (held_count, page_rows, pair_width)
    raw_far, met[1] = lax.optimization_barrier((raw_far, met[1]))
    listed_pages = deliver(pick_pages((raw.reshape(page_shape), raw_far.reshape(page_shape)), chosen))

    new_count = page_table.shape[1]
    page_tiles = page_width // LANES
    tags = jnp.broadcast_to(page_table.reshape(new_count, 1, 1).astype(new_latent.dtype), (new_count, 16, LANES))
    tagged = jnp.concatenate([new_latent.reshape(new_count, page_tiles, LANES), tags], axis=1)
    tagged, raw_far = lax.optimization_barrier((tagged, raw_far))
    tagged_far = lax.ppermute(tagged, "dp", across)

    met, tagged_far = lax.optimization_barrier((met, tagged_far))
    turned = turn(met)
    arrived = [turned[0]] + [lax.ppermute(turned[k], "expert", along(k * side)) for k in range(1, side)]

    holders = listed // held_count
    rank = jnp.minimum(earlier_same(holders), PAIR - 1)
    across_half = (half_of(holders) != half_of(me)).astype(jnp.int32)
    place = (seat_of(holders) * 2 + across_half) * PAIR + rank
    context = attend(queries, new_latent, (listed_pages,), place)

    groups = (token_expert // EXP_GROUP).reshape(-1)
    slot = (groups ^ here) * capacity + earlier_same(groups)

    both = jnp.concatenate([tagged, tagged_far], axis=0)
    seat = jnp.arange(seats, dtype=jnp.int32)
    owner = (seat // 2) * 4 + half_of(me) * 2 + seat % 2
    wanted = (owner[:, None] * new_count + jnp.arange(new_count, dtype=jnp.int32)).reshape(-1)
    source = first_match(wanted, both[:, page_tiles, 0].astype(jnp.int32))
    picked = pick_pages((both,), source)
    picked, listed_pages, arrived[3] = lax.optimization_barrier((picked, listed_pages, arrived[3]))
    pages = deliver(picked)
    tagged_as = pages[:, page_tiles, 0].astype(jnp.int32)
    source = first_match(me * new_count + jnp.arange(new_count, dtype=jnp.int32), tagged_as)
    decode_pool = pick_pages((pages,), source, page_tiles).reshape(1, new_count, page_width)
    slot, context, decode_pool = lax.optimization_barrier((slot, context, decode_pool))
    moe_out = combine(slot[:, None], gate, arrived, parts)
    return (context, moe_out, decode_pool)


def solution(mesh):
    return jax.shard_map(
        shards,
        mesh=mesh,
        in_specs=(
            P(("expert", "dp"), None),
            P(("expert", "dp"), None),
            P("expert", "dp", None),
            P(("expert", "dp"), None),
            P(("expert", "dp"), None),
            P(("expert", "dp"), None),
            P("expert", "dp", None, None, None),
            P("expert", "dp"),
        ),
        out_specs=(P(("expert", "dp"), None), P(("expert", "dp"), None), P("expert", "dp", None)),
        check_vma=False,
    )
```

```python
import functools

import jax
import jax.numpy as jnp
from jax import lax
from jax.experimental import pallas as pl
from jax.experimental.pallas import tpu as pltpu
from jax.sharding import PartitionSpec as P

EXP_GROUP = 24
LAT = 512
PAIR = 2
LANES = 128

exp2_scale = 0.07216878364870322 * 1.4426950408889634


def pick_kernel(index_ref, *refs):
    page_refs, out_ref = refs[:-1], refs[-1]
    each, count = len(page_refs), index_ref.shape[0]
    for i in range(count):
        out_ref[i] = page_refs[i // PAIR % each][index_ref[i], : out_ref.shape[1]]


def pick_pages(sources, index, rows=None):
    width = sources[0].shape[2]
    rows = rows or sources[0].shape[1]
    return pl.pallas_call(
        pick_kernel,
        out_shape=jax.ShapeDtypeStruct((index.shape[0], rows, width), sources[0].dtype),
        in_specs=[pl.BlockSpec(memory_space=pltpu.SMEM)] + [pl.BlockSpec(memory_space=pltpu.VMEM)] * len(sources),
        out_specs=pl.BlockSpec(memory_space=pltpu.VMEM),
        compiler_params=pltpu.CompilerParams(vmem_limit_bytes=16 * 2**20),
        name="pick_pages",
    )(index, *sources)


def attend_kernel(step_pairs, width, blocks, place_ref, q_ref, own_ref, *refs):
    block_refs, (out_ref, held, low, high, sems) = refs[:blocks], refs[blocks:]
    count = place_ref.shape[0]
    each, page_rows, pair_width = block_refs[0].shape
    span = low.shape[1]
    shift = span - width
    tokens = own_ref.shape[0]
    half = count * page_rows
    prefix = 2 * half

    @pl.when(pl.program_id(0) == 0)
    def _():
        def move(i):
            return pltpu.make_async_copy(block_refs[i], held.at[pl.ds(each * i, each)], sems.at[i])

        for i in range(blocks):
            move(i).start()

        own = own_ref[...]
        empty = jnp.zeros((tokens, shift), own.dtype)
        low[prefix:, :] = jnp.concatenate([own, empty], axis=1)
        high[prefix:, :] = jnp.concatenate([empty, own], axis=1)
        lane = lax.broadcasted_iota(jnp.int32, (page_rows, span), 1)
        for i in range(blocks):
            move(i).wait()
        for i in range(count):
            place = place_ref[i]
            first = jnp.where(lane < width, held[place, :, :span].astype(jnp.float32), 0.0)
            second = jnp.where(lane >= shift, held[place, :, pair_width - span :].astype(jnp.float32), 0.0)
            evens = pl.ds(i * page_rows, page_rows)
            odds = pl.ds(half + i * page_rows, page_rows)
            low[evens, :] = first.astype(low.dtype)
            high[evens, :] = pltpu.roll(first, shift, 1).astype(low.dtype)
            low[odds, :] = pltpu.roll(second, width, 1).astype(low.dtype)
            high[odds, :] = second.astype(low.dtype)

    contract = (((1,), (1,)), ((), ()))
    rows = step_pairs * tokens
    token = lax.broadcasted_iota(jnp.int32, (rows, tokens), 0) % tokens
    visible = lax.broadcasted_iota(jnp.int32, (rows, tokens), 1) <= token
    for parity, keys in ((0, low), (1, high)):
        offset = parity * (pair_width - span)
        q = jnp.concatenate(
            [q_ref[:, p * pair_width + offset : p * pair_width + offset + span] for p in range(step_pairs)], axis=0
        )
        before = lax.dot_general(q, keys[:prefix, :], contract, preferred_element_type=jnp.float32)
        own = lax.dot_general(q, keys[prefix:, :], contract, preferred_element_type=jnp.float32)
        own = jnp.where(visible, own, -jnp.inf)
        largest = jnp.maximum(jnp.max(before, axis=1, keepdims=True), jnp.max(own, axis=1, keepdims=True))
        before = jnp.exp2((before - largest) * exp2_scale)
        own = jnp.exp2((own - largest) * exp2_scale)
        total = jnp.sum(before, axis=1, keepdims=True) + jnp.sum(own, axis=1, keepdims=True)
        mixed = jnp.dot(before.astype(low.dtype), low[:prefix, :LAT], preferred_element_type=jnp.float32)
        mixed += jnp.dot(own.astype(low.dtype), low[prefix:, :LAT], preferred_element_type=jnp.float32)
        mixed = (mixed / total).astype(out_ref.dtype)
        for p in range(step_pairs):
            head = 2 * p + parity
            out_ref[:, head * LAT : (head + 1) * LAT] = mixed[p * tokens : (p + 1) * tokens]


def attend(queries, own, blocks, place):
    tokens, width = own.shape
    _, page_rows, pair_width = blocks[0].shape
    count = place.shape[0]
    span = -(-width // LANES) * LANES
    pairs = queries.shape[1] // pair_width
    step_pairs = 4
    keys = count * page_rows * 2 + tokens
    heads = 2 * pairs
    return pl.pallas_call(
        functools.partial(attend_kernel, step_pairs, width, len(blocks)),
        out_shape=jax.ShapeDtypeStruct((tokens, heads * LAT), queries.dtype),
        grid=(pairs // step_pairs,),
        in_specs=[
            pl.BlockSpec(memory_space=pltpu.SMEM),
            pl.BlockSpec((tokens, step_pairs * pair_width), lambda i: (0, i)),
            pl.BlockSpec((tokens, width), lambda i: (0, 0)),
        ]
        + [pl.BlockSpec(memory_space=pl.ANY)] * len(blocks),
        out_specs=pl.BlockSpec((tokens, 2 * step_pairs * LAT), lambda i: (0, i)),
        scratch_shapes=[
            pltpu.VMEM((len(blocks) * blocks[0].shape[0], page_rows, pair_width), queries.dtype),
            pltpu.VMEM((keys, span), queries.dtype),
            pltpu.VMEM((keys, span), queries.dtype),
            pltpu.SemaphoreType.DMA((len(blocks),)),
        ],
        compiler_params=pltpu.CompilerParams(vmem_limit_bytes=56 * 2**20),
        cost_estimate=pl.CostEstimate(
            flops=2 * tokens * heads * keys * (width + LAT),
            bytes_accessed=2 * tokens * heads * (width + LAT),
            transcendentals=tokens * heads * keys,
        ),
        name="attend",
    )(place, queries, own, *blocks)


def pack_kernel(groups, parts, here_ref, rows_ref, *refs):
    out_refs, stack = refs[:-1], refs[-1]
    count, width = rows_ref.shape
    part_width = width // parts
    for part in range(parts):
        stack[pl.ds(part * count, count), :] = rows_ref[:, part * part_width : (part + 1) * part_width]
    side = len(out_refs)
    block = count // groups * parts
    depth = parts * count
    row = lax.broadcasted_iota(jnp.int32, (side * block, 1), 0)
    k = row // block
    slot = (row - k * block) // parts
    part = row % parts
    column = lax.broadcasted_iota(jnp.int32, (side * block, depth), 1)
    for far in range(side):
        group = (k * side + far) ^ here_ref[0]
        picker = (column == part * count + slot * groups + group).astype(stack.dtype)
        out_refs[far][...] = jnp.dot(picker, stack[...], preferred_element_type=jnp.float32).astype(stack.dtype)


def pack_rows(rows, here, groups, side, parts):
    count, width = rows.shape
    out = jax.ShapeDtypeStruct((count * parts // side, width // parts), rows.dtype)
    return pl.pallas_call(
        functools.partial(pack_kernel, groups, parts),
        out_shape=(out,) * side,
        in_specs=[pl.BlockSpec(memory_space=pltpu.SMEM), pl.BlockSpec(memory_space=pltpu.VMEM)],
        out_specs=(pl.BlockSpec(memory_space=pltpu.VMEM),) * side,
        scratch_shapes=[pltpu.VMEM((count * parts, width // parts), rows.dtype)],
        compiler_params=pltpu.CompilerParams(vmem_limit_bytes=32 * 2**20),
        cost_estimate=pl.CostEstimate(
            flops=2 * count * parts * count * width, bytes_accessed=4 * count * width, transcendentals=0
        ),
        name="pack_rows",
    )(here, rows)


def turn_kernel(*refs):
    side = len(refs) // 2
    share = refs[0].shape[0] // side
    for k in range(side):
        for far in range(side):
            refs[side + k][pl.ds(far * share, share), :] = refs[far][pl.ds(k * share, share), :]


def turn(blocks):
    side = len(blocks)
    return pl.pallas_call(
        turn_kernel,
        out_shape=(jax.ShapeDtypeStruct(blocks[0].shape, blocks[0].dtype),) * side,
        in_specs=[pl.BlockSpec(memory_space=pltpu.VMEM)] * side,
        out_specs=(pl.BlockSpec(memory_space=pltpu.VMEM),) * side,
        compiler_params=pltpu.CompilerParams(vmem_limit_bytes=16 * 2**20),
        name="turn",
    )(*blocks)


def combine_kernel(parts, slot_ref, gate_ref, *refs):
    row_refs, (out_ref, rows, sems) = refs[:-3], refs[-3:]
    tokens = slot_ref.shape[0]
    depth, part_width = rows.shape
    shares = [ref.shape[0] for ref in row_refs]

    def move(i):
        return pltpu.make_async_copy(row_refs[i], rows.at[pl.ds(sum(shares[:i]), shares[i])], sems.at[i])

    for i in range(len(row_refs)):
        move(i).start()
    column = lax.broadcasted_iota(jnp.int32, (tokens, depth), 1)
    first = slot_ref[...] * parts
    picker = jnp.concatenate([(column == first + part).astype(rows.dtype) for part in range(parts)], axis=0)
    gate = gate_ref[...]
    for i in range(len(row_refs)):
        move(i).wait()
    picked = jnp.dot(picker, rows[...], preferred_element_type=jnp.float32)
    for part in range(parts):
        out_ref[:, part * part_width : (part + 1) * part_width] = (
            picked[part * tokens : (part + 1) * tokens] * gate
        ).astype(out_ref.dtype)


def combine(slot, gate, arrived, parts):
    tokens = slot.shape[0]
    depth = sum(block.shape[0] for block in arrived)
    part_width = arrived[0].shape[1]
    return pl.pallas_call(
        functools.partial(combine_kernel, parts),
        out_shape=jax.ShapeDtypeStruct((tokens, parts * part_width), arrived[0].dtype),
        in_specs=[pl.BlockSpec(memory_space=pltpu.VMEM)] * 2 + [pl.BlockSpec(memory_space=pl.ANY)] * len(arrived),
        out_specs=pl.BlockSpec(memory_space=pltpu.VMEM),
        scratch_shapes=[
            pltpu.VMEM((depth, part_width), arrived[0].dtype),
            pltpu.SemaphoreType.DMA((len(arrived),)),
        ],
        compiler_params=pltpu.CompilerParams(vmem_limit_bytes=40 * 2**20),
        cost_estimate=pl.CostEstimate(
            flops=2 * parts * tokens * depth * part_width,
            bytes_accessed=2 * (depth + tokens * parts) * part_width,
            transcendentals=0,
        ),
        name="combine",
    )(slot, gate, *arrived)


def earlier_same(groups):
    count = groups.shape[0]
    order = jnp.arange(count, dtype=jnp.int32)
    same = (groups[None, :] == groups[:, None]) & (order[None, :] < order[:, None])
    return jnp.sum(same.astype(jnp.int32), axis=1)


def first_match(wanted, values):
    hit = wanted[:, None] == values[None, :]
    order = jnp.arange(values.shape[0], dtype=jnp.int32)
    first = jnp.min(jnp.where(hit, order[None, :], values.shape[0]), axis=1)
    return jnp.where(first < values.shape[0], first, 0)


def shards(queries, new_latent, held_pages, page_list, token_expert, gate, expert_rows, page_table):
    groups_here = lax.axis_size("expert")
    dp_size = lax.axis_size("dp")
    me = lax.axis_index("dp")
    held_count, page_width = held_pages.shape[1:]
    entry_width = new_latent.shape[1]
    pair_width = 2 * entry_width
    page_rows = page_width // pair_width
    half_of = lambda i: (i // 2) % 2
    seat_of = lambda i: (i // 4) * 2 + i % 2
    halves = [[i for i in range(dp_size) if half_of(i) == z] for z in range(2)]
    across = [(i, i ^ 2) for i in range(dp_size)]
    seats = dp_size // 2

    raw = held_pages[0]
    raw_far = lax.ppermute(raw, "dp", across)

    listed = page_list.reshape(-1)
    count = listed.shape[0]
    here = lax.axis_index("expert")
    capacity, width = expert_rows.shape[3:]
    parts = 8
    side = 4
    along = lambda k: [(i, i ^ k) for i in range(groups_here)]
    rows = jnp.transpose(expert_rows[0, 0], (1, 0, 2)).reshape(capacity * groups_here, width)
    packed = pack_rows(rows, here.reshape(1).astype(jnp.int32), groups_here, side, parts)
    packed, listed = lax.optimization_barrier((packed, listed))
    lists = lax.all_to_all(
        jnp.broadcast_to(listed[None], (seats, count)), "dp", 0, 0, axis_index_groups=halves, tiled=True
    )

    order = jnp.arange(count, dtype=jnp.int32)
    mine = (lists // held_count)[:, None, :] == jnp.stack([me, me ^ 2])[None, :, None]
    rank = jnp.sum((mine[:, :, None, :] & (order[None, :] < order[:, None])).astype(jnp.int32), axis=3)
    slots = jnp.arange(PAIR, dtype=jnp.int32)
    hit = mine[:, :, None, :] & (rank[:, :, None, :] == slots[:, None])
    chosen = jnp.sum(jnp.where(hit, (lists % held_count)[:, None, None, :], 0), axis=3).reshape(-1)

    def deliver(picked):
        blocks = picked.reshape(seats, -1, picked.shape[2])
        arrived = lax.all_to_all(blocks, "dp", 0, 0, axis_index_groups=halves, tiled=True)
        return arrived.reshape(picked.shape)

    met = [packed[0]] + [lax.ppermute(packed[far], "expert", along(far)) for far in range(1, side)]
    page_shape = (held_count, page_rows, pair_width)
    raw_far, met[1] = lax.optimization_barrier((raw_far, met[1]))
    listed_pages = deliver(pick_pages((raw.reshape(page_shape), raw_far.reshape(page_shape)), chosen))

    new_count = page_table.shape[1]
    page_tiles = page_width // LANES
    tags = jnp.broadcast_to(page_table.reshape(new_count, 1, 1).astype(new_latent.dtype), (new_count, 16, LANES))
    tagged = jnp.concatenate([new_latent.reshape(new_count, page_tiles, LANES), tags], axis=1)
    tagged_far = lax.ppermute(tagged, "dp", across)

    met, tagged_far = lax.optimization_barrier((met, tagged_far))
    turned = turn(met)
    early = turned[3].shape[0] * 3 // 4 // 16 * 16
    arrived = [turned[0]] + [lax.ppermute(turned[k], "expert", along(k * side)) for k in range(1, side - 1)]
    arrived += [lax.ppermute(half, "expert", along(3 * side)) for half in (turned[3][:early], turned[3][early:])]

    holders = listed // held_count
    rank = jnp.minimum(earlier_same(holders), PAIR - 1)
    across_half = (half_of(holders) != half_of(me)).astype(jnp.int32)
    place = (seat_of(holders) * 2 + across_half) * PAIR + rank
    context = attend(queries, new_latent, (listed_pages,), place)

    groups = (token_expert // EXP_GROUP).reshape(-1)
    slot = (groups ^ here) * capacity + earlier_same(groups)

    both = jnp.concatenate([tagged, tagged_far], axis=0)
    seat = jnp.arange(seats, dtype=jnp.int32)
    owner = (seat // 2) * 4 + half_of(me) * 2 + seat % 2
    wanted = (owner[:, None] * new_count + jnp.arange(new_count, dtype=jnp.int32)).reshape(-1)
    source = first_match(wanted, both[:, page_tiles, 0].astype(jnp.int32))
    picked = pick_pages((both,), source)
    picked, listed_pages, arrived[3] = lax.optimization_barrier((picked, listed_pages, arrived[3]))
    pages = deliver(picked)
    tagged_as = pages[:, page_tiles, 0].astype(jnp.int32)
    source = first_match(me * new_count + jnp.arange(new_count, dtype=jnp.int32), tagged_as)
    decode_pool = pick_pages((pages,), source, page_tiles).reshape(1, new_count, page_width)
    slot, context, decode_pool = lax.optimization_barrier((slot, context, decode_pool))
    moe_out = combine(slot[:, None], gate, arrived, parts)
    return (context, moe_out, decode_pool)


def solution(mesh):
    return jax.shard_map(
        shards,
        mesh=mesh,
        in_specs=(
            P(("expert", "dp"), None),
            P(("expert", "dp"), None),
            P("expert", "dp", None),
            P(("expert", "dp"), None),
            P(("expert", "dp"), None),
            P(("expert", "dp"), None),
            P("expert", "dp", None, None, None),
            P("expert", "dp"),
        ),
        out_specs=(P(("expert", "dp"), None), P(("expert", "dp"), None), P("expert", "dp", None)),
        check_vma=False,
    )
```
